32 devices in a mesh: dp: 8 (over z, core), fsdp: 4 (over y, x).
Axes of the slice: x: 2, y: 2, z: 4, core: 2. Of those that a mesh axis runs over, the one named last changes fastest.
Arguments:
- normed: bfloat16 [12288, 4096], P(('dp', 'fsdp')), may hold values from -6 to 6
- queries: bfloat16 [12288, 2048], P(('dp', 'fsdp')), may hold values from -48 to 48
- key_rows: bfloat16 [12288, 512], P(('dp', 'fsdp')), may hold values from -6 to 6
- out_grad: bfloat16 [12288, 2048], P(('dp', 'fsdp')), may hold values from -6 to 6
- value_weight: bfloat16 [4096, 512], P('fsdp'), may hold values from -0.09375 to 0.09375
- doc_ids: int32 [32, 384], P(('dp', 'fsdp')), may hold values from 0 to 3, never falling along the last dimension, each value on 1 to 256 neighbouring positions
- send_to: int32 [32, 8], P(('dp', 'fsdp')), may hold values from 0 to 7, as said below
- take_from: int32 [32, 8], P(('dp', 'fsdp')), may hold values from 0 to 7, as said below
Outputs:
- query_grad: bfloat16 [12288, 2048], P(('dp', 'fsdp'))
- key_grad: bfloat16 [12288, 512], P(('dp', 'fsdp'))
- input_grad: bfloat16 [12288, 4096], P(('dp', 'fsdp'))
- weight_grad: float32 [4096, 512], P(('dp', 'fsdp'))
The draws below stay inside these ranges and needn't reach their ends.
Inputs may be any that keep to these rules, and one draw needn't show every extreme that they name: `send_to`: entry b of a device's row names the dp index of the device, with the same fsdp index, that packs this device's rows b * 48 to (b + 1) * 48 - 1; the 8 entries of a row are distinct, and every device packs exactly 8 blocks. `take_from`: entry p of a device's row names the dp index of the device whose block, sent to this device by send_to, becomes this device's packed rows p * 48 to (p + 1) * 48 - 1; the entries of a row are distinct, so one device sends at most one block to another. `doc_ids`: along a device's 384 rows document numbers never fall; a document holds at most 256 rows, and one document in every draw holds exactly that many.
All inputs are finite; a program needn't handle non-finite values.
Results may differ from the reference program's by a relative error of at most 0.006.
Values may be sent and summed in bfloat16 or wider, within the bound.
A program may use at most 128 MiB of HBM per device.

```python
import math
import jax
import jax.numpy as jnp
import numpy as np
from jax import lax

D = 4096
HEADS = 16
KV_HEADS = 4
HEAD_DIM = 128
BLOCK_ROWS = 48
BLOCKS = 8
ROWS = 384
TOKENS = 12288
N_DP = 8
N_FSDP = 4


def random_perm(subkey, count_rows, width):
    scores = jax.random.randint(subkey, (count_rows, width), 0, 1 << 20) * width + jnp.arange(width, dtype=jnp.int32)[None, :]
    return jnp.argsort(scores, axis=1).astype(jnp.int32)


def plan_tables(key):
    source_perm = random_perm(jax.random.fold_in(key, 21), N_FSDP, N_DP)
    dest_perm = random_perm(jax.random.fold_in(key, 22), N_FSDP, N_DP)
    offsets = random_perm(jax.random.fold_in(key, 23), N_FSDP, N_DP)[:, :BLOCKS]
    source_inv = jnp.argsort(source_perm, axis=1).astype(jnp.int32)
    dest_inv = jnp.argsort(dest_perm, axis=1).astype(jnp.int32)
    position = (source_perm[:, :, None] + offsets[:, None, :]) % N_DP
    sending = jnp.take_along_axis(dest_perm, position.reshape(N_FSDP, N_DP * BLOCKS), axis=1).reshape(N_FSDP, N_DP, BLOCKS)
    send_table = jnp.transpose(sending, (1, 0, 2)).reshape(N_DP * N_FSDP, BLOCKS)
    back_pos = (dest_inv[:, :, None] - offsets[:, None, :]) % N_DP
    sources = jnp.take_along_axis(source_inv, back_pos.reshape(N_FSDP, N_DP * BLOCKS), axis=1).reshape(N_FSDP, N_DP, BLOCKS)
    slot_perm = random_perm(jax.random.fold_in(key, 24), N_FSDP * N_DP, BLOCKS).reshape(N_FSDP, N_DP, BLOCKS)
    taking = jnp.take_along_axis(sources, slot_perm, axis=2)
    take_table = jnp.transpose(taking, (1, 0, 2)).reshape(N_DP * N_FSDP, BLOCKS)
    return (send_table.astype(jnp.int32), take_table.astype(jnp.int32))


def base_keys(key):
    drawn = jnp.clip(jax.random.normal(jax.random.fold_in(key, 31), (TOKENS, KV_HEADS * HEAD_DIM), jnp.float32), -6.0, 6.0)
    return drawn


def draw_key_rows(key, part):
    return base_keys(key).astype(jnp.bfloat16)


def draw_queries(key, part):
    drawn = jnp.clip(jax.random.normal(jax.random.fold_in(key, 32), (TOKENS, HEADS * HEAD_DIM), jnp.float32), -6.0, 6.0)
    return drawn.astype(jnp.bfloat16)


def draw_send_to(key, part):
    return plan_tables(key)[0]


def draw_take_from(key, part):
    return plan_tables(key)[1]


def raised(result, key, source, target, parts, factor):
    def block_of(axis_at):
        return (jnp.arange(result.shape[axis_at]) // (result.shape[axis_at] // parts)).reshape((-1,) + (1,) * (result.ndim - 1 - axis_at))

    first = jax.random.permutation(key, parts)[block_of(target)]
    second = (block_of(target) + parts // 2) % parts
    return jnp.where((block_of(source) == first) | (block_of(source) == second), factor * result, result)


def levels(key, shape, split, smallest, largest):
    factor_of, own = 1.0, jax.random.fold_in(key, 6)
    for axis_at, blocks in split:
        heights = jnp.exp(jax.random.uniform(jax.random.fold_in(own, axis_at), (blocks,), jnp.float32, smallest / len(split), largest / len(split)))
        factor_of = factor_of * jnp.repeat(heights, shape[axis_at] // blocks).reshape([-1 if axis == axis_at else 1 for axis in range(len(shape))])
    return factor_of


def length_profile(number_of, total, limit, skew):
    loads = [(1 << 20) // math.isqrt(grade ** skew) + 1 for grade in range(2, number_of + 1)]
    spare, given = total - limit - (number_of - 1), [1] * (number_of - 1)
    while spare > 0:
        candidates = [i for i in range(number_of - 1) if given[i] < limit]
        pool, left = sum([loads[i] for i in candidates]), spare
        for i in candidates:
            extra = min(limit - given[i], max(1, left * loads[i] // pool), spare)
            given[i] = given[i] + extra
            spare = spare - extra
    return np.array([limit] + given)


def ragged_sizes(stream_key, amount, total, most, skew):
    if amount == 2:
        one = jax.random.randint(stream_key, (), max(1, total - most), min(most, total - 1) + 1)
        return jnp.stack([one, total - one])
    tallies = jnp.asarray(length_profile(amount, total, most, skew), jnp.int32)
    pairs = (amount - 1) // 2
    source_of, sink = tallies[1:1 + 2 * pairs:2], tallies[2:2 + 2 * pairs:2]
    margin = jnp.minimum(source_of - 1, most - sink)
    shifted = jax.random.randint(jax.random.fold_in(stream_key, 1), (pairs,), 0, 1 << 20) % (margin + 1)
    tallies = tallies.at[1:1 + 2 * pairs:2].set(source_of - shifted).at[2:2 + 2 * pairs:2].set(sink + shifted)
    return tallies[jax.random.permutation(jax.random.fold_in(stream_key, 2), amount)]


def centred(own_key, extent, spread, bound, shards=(), kind=jnp.bfloat16):
    gain = levels(own_key, extent, shards, -0.22, 0.18) if shards else 1.0
    values = jax.random.normal(own_key, extent, jnp.float32) * spread * gain
    return jnp.minimum(jnp.maximum(values, -bound), bound).astype(kind)


def noise_with(own_key, dims, scale, most, split, heavy, kind=jnp.bfloat16):
    values = scale * jax.random.normal(own_key, dims, jnp.float32)
    if split:
        values = values * levels(own_key, dims, split, -0.22, 0.18)
    return jnp.clip(raised(values, jax.random.fold_in(own_key, 3), *heavy), -most, most).astype(kind)


def setup_inputs(seed: int = 0) -> dict:
    key_of = jax.random.split(jax.random.key(seed), 9)
    return {
        "normed": noise_with(key_of[0], (TOKENS, D), 1.0, 6.0, ((0, 32),), (0, 1, 32, 2.75)),
        "queries": draw_queries(jax.random.fold_in(key_of[8], 71), 0),
        "key_rows": draw_key_rows(jax.random.fold_in(key_of[8], 71), 0),
        "out_grad": centred(key_of[3], (TOKENS, HEADS * HEAD_DIM), 1.0, 6.0, ((0, 32),)),
        "value_weight": centred(key_of[4], (D, KV_HEADS * HEAD_DIM), D ** -0.5, 0.09375, ((0, 4),)),
        "doc_ids": jax.vmap(lambda own: jnp.searchsorted(jnp.cumsum(ragged_sizes(own, 4, ROWS, 2 * ROWS // 3, 2)), jnp.arange(ROWS), side="right"))(jax.random.split(key_of[5], (N_DP * N_FSDP))).reshape((N_DP * N_FSDP, ROWS)).astype(jnp.int32),
        "send_to": draw_send_to(jax.random.fold_in(key_of[8], 71), 0),
        "take_from": draw_take_from(jax.random.fold_in(key_of[8], 71), 0),
    }


def reference(normed, queries, key_rows, out_grad, value_weight, doc_ids, send_to, take_from):
    group_size = HEADS // KV_HEADS
    score_scale = HEAD_DIM ** -0.5
    device_count = N_DP * N_FSDP
    values = jnp.dot(normed, value_weight, preferred_element_type=jnp.float32).astype(jnp.bfloat16)
    send_tab = send_to.reshape(N_DP, N_FSDP, BLOCKS)
    take_tab = take_from.reshape(N_DP, N_FSDP, BLOCKS)
    fsdp_index = jnp.arange(N_FSDP, dtype=jnp.int32)[None, :, None]
    dp_index = jnp.arange(N_DP, dtype=jnp.int32)[:, None, None]
    block_index = jnp.arange(BLOCKS, dtype=jnp.int32)
    source_rows = send_tab[take_tab, fsdp_index]
    source_block = jnp.sum(jnp.where(source_rows == dp_index[..., None], block_index, 0), axis=-1).astype(jnp.int32)
    dest_rows = take_tab[send_tab, fsdp_index]
    dest_block = jnp.sum(jnp.where(dest_rows == dp_index[..., None], block_index, 0), axis=-1).astype(jnp.int32)

    def to_packed(array):
        shaped = array.reshape(N_DP, N_FSDP, BLOCKS, BLOCK_ROWS, array.shape[1])
        return shaped[take_tab, fsdp_index, source_block].reshape(array.shape)

    def to_generator(array):
        shaped = array.reshape(N_DP, N_FSDP, BLOCKS, BLOCK_ROWS, array.shape[1])
        return shaped[send_tab, fsdp_index, dest_block].reshape(array.shape)

    packed_q = to_packed(queries)
    packed_k = to_packed(key_rows)
    packed_v = to_packed(values)

    def device_attention(inputs):
        dev_q, dev_k, dev_v, dev_grad, doc_row = inputs
        query_heads = dev_q.astype(jnp.float32).reshape(ROWS, KV_HEADS, group_size, HEAD_DIM)
        grad_heads = dev_grad.astype(jnp.float32).reshape(ROWS, KV_HEADS, group_size, HEAD_DIM)
        key_heads = dev_k.astype(jnp.float32).reshape(ROWS, KV_HEADS, HEAD_DIM)
        value_heads = dev_v.astype(jnp.float32).reshape(ROWS, KV_HEADS, HEAD_DIM)
        scores = jnp.einsum("igxd,jgd->gxij", query_heads, key_heads) * score_scale
        positions = jnp.arange(ROWS, dtype=jnp.int32)
        allowed = (doc_row[:, None] == doc_row[None, :]) & (positions[None, :] <= positions[:, None])
        masked = jnp.where(allowed, scores, -jnp.inf)
        row_peak = jnp.max(masked, axis=-1, keepdims=True)
        exponent = jnp.exp(masked - row_peak)
        attn_probs = exponent / jnp.sum(exponent, axis=-1, keepdims=True)
        probs_half = attn_probs.astype(jnp.bfloat16).astype(jnp.float32)
        attn_out = jnp.einsum("gxij,jgd->igxd", probs_half, value_heads)
        delta_rows = jnp.sum(grad_heads * attn_out, axis=-1)
        prob_grad = jnp.einsum("igxd,jgd->gxij", grad_heads, value_heads)
        score_grad = (attn_probs * (prob_grad - jnp.transpose(delta_rows, (1, 2, 0))[..., None]) * score_scale)
        score_grad = score_grad.astype(jnp.bfloat16).astype(jnp.float32)
        query_grad = jnp.einsum("gxij,jgd->igxd", score_grad, key_heads).astype(jnp.bfloat16).reshape(ROWS, -1)
        key_grad = jnp.einsum("gxij,igxd->jgd", score_grad, query_heads).astype(jnp.bfloat16).reshape(ROWS, -1)
        value_grad = jnp.einsum("gxij,igxd->jgd", probs_half, grad_heads).astype(jnp.bfloat16).reshape(ROWS, -1)
        return query_grad, key_grad, value_grad

    results = lax.map(device_attention, (packed_q.reshape(device_count, ROWS, -1), packed_k.reshape(device_count, ROWS, -1), packed_v.reshape(device_count, ROWS, -1), out_grad.reshape(device_count, ROWS, -1), doc_ids))
    query_grad = results[0].reshape(TOKENS, -1)
    key_grad = results[1].reshape(TOKENS, -1)
    value_grad = results[2].reshape(TOKENS, -1)
    input_grad = jnp.dot(value_grad, value_weight.T, preferred_element_type=jnp.float32).astype(jnp.bfloat16)
    value_home = to_generator(value_grad)
    weight_grad = jnp.dot(normed.T, value_home, preferred_element_type=jnp.float32) * (TOKENS ** -0.5)
    return query_grad, key_grad, input_grad, weight_grad
```

```python
import functools

import jax
import jax.numpy as jnp
from jax import lax
from jax.experimental import pallas as pl
from jax.experimental.pallas import tpu as pltpu
from jax.sharding import PartitionSpec as P

HEADS = 16
KV_HEADS = 4
HEAD_DIM = 128
GROUP = HEADS // KV_HEADS
GROUP_COLS = GROUP * HEAD_DIM
KV_COLS = KV_HEADS * HEAD_DIM
BLOCK_ROWS = 48
TILE = 128
HALF_COLS = KV_COLS // 2
MASKED = -1e30
MESH = pl.DeviceIdType.MESH
CH_K, CH_V, CH_Q, CH_G = 0, 1, 2, 2 + KV_HEADS
NT = (((1,), (1,)), ((), ()))
TN = (((0,), (0,)), ((), ()))


def kernel(
    n_dp, n_f, grad_scale,
    normed, queries, keys, out_grad, weight, doc_row, send_to, take_from, send_block, take_block,
    query_grad, key_grad, input_grad, weight_grad,
    tx, rx, gtx, grx, whole_w, values_f32, values, packed_q, packed_k, packed_v,
    normed_t, bias, dk_acc, dv_acc, value_grad, home, pair_tx, pair_rx, pair_sum,
    f_rx, z_tx, z_rx,
    a_send, a_recv, w_send, w_recv, ws_send, ws_recv, p_send, p_recv, f_send, f_recv,
    z_send, z_recv,
):
    rows, width = normed.shape
    blocks = rows // BLOCK_ROWS
    n_z = n_dp // 2
    shard = width // n_f
    half = shard // 2
    dest_rows = width // n_dp
    piece = dest_rows // n_f
    d = lax.axis_index("dp")
    f = lax.axis_index("fsdp")
    core = lax.rem(d, 2)
    z = lax.div(d, 2)
    sibling = d + 1 - 2 * core

    def dp_peer(i):
        return lax.rem(d + i, n_dp)

    def f_peer(i):
        return lax.rem(f + i, n_f)

    barrier = pltpu.get_barrier_semaphore()

    def greet_dp(i, _):
        pl.semaphore_signal(barrier, inc=1, device_id={"dp": dp_peer(i)}, device_id_type=MESH)
        return 0

    def greet_f(i, _):
        pl.semaphore_signal(barrier, inc=1, device_id={"fsdp": f_peer(i)}, device_id_type=MESH)
        return 0

    lax.fori_loop(1, n_dp, greet_dp, 0)
    lax.fori_loop(1, n_f, greet_f, 0)

    def to_slots(source, column, cols, table, out, own):
        def body(p, _):
            out[p] = source[table[0, p], :, column : column + cols]
            return 0

        lax.fori_loop(0, n_dp, body, 0)
        own[d] = out[d]

    def from_slots(landed, table, out, column, cols):
        for p in range(blocks):
            out[p * BLOCK_ROWS : (p + 1) * BLOCK_ROWS, column : column + cols] = landed[table[0, p]]

    def exchange(channel, out, landed, i):
        to = dp_peer(i)
        return pltpu.make_async_remote_copy(
            src_ref=out.at[to],
            dst_ref=landed.at[d],
            send_sem=a_send.at[channel, to],
            recv_sem=a_recv.at[channel, d],
            device_id={"dp": to},
            device_id_type=MESH,
        )

    def arrival(channel, out, landed, i):
        source = dp_peer(i)
        return pltpu.make_async_remote_copy(
            src_ref=out.at[source],
            dst_ref=landed.at[source],
            send_sem=a_send.at[channel, source],
            recv_sem=a_recv.at[channel, source],
            device_id={"dp": source},
            device_id_type=MESH,
        )

    def each(low, high, act):
        def body(i, _):
            act(i)
            return 0

        lax.fori_loop(low, high, body, 0)

    def send_all(channel, out, landed):
        each(1, n_dp, lambda i: exchange(channel, out, landed, i).start())

    def recv_all(channel, out, landed):
        each(1, n_dp, lambda i: arrival(channel, out, landed, i).wait_recv())

    def w_copy(i):
        to = f_peer(i)
        return pltpu.make_async_remote_copy(
            src_ref=weight.at[pl.ds(pl.multiple_of(core * half, 16), half)],
            dst_ref=whole_w.at[f, core],
            send_sem=w_send.at[to],
            recv_sem=w_recv.at[f],
            device_id={"fsdp": to},
            device_id_type=MESH,
        )

    def w_arrival(i):
        source = f_peer(i)
        return pltpu.make_async_remote_copy(
            src_ref=weight.at[pl.ds(pl.multiple_of(core * half, 16), half)],
            dst_ref=whole_w.at[source, core],
            send_sem=w_send.at[source],
            recv_sem=w_recv.at[source],
            device_id={"fsdp": source},
            device_id_type=MESH,
        )

    def w_forward(i):
        source = f_peer(i)
        return pltpu.make_async_remote_copy(
            src_ref=whole_w.at[source, core],
            dst_ref=whole_w.at[source, core],
            send_sem=ws_send.at[source],
            recv_sem=ws_recv.at[source],
            device_id={"dp": sibling},
            device_id_type=MESH,
        )

    def w_forwarded(i):
        source = f_peer(i)
        return pltpu.make_async_remote_copy(
            src_ref=whole_w.at[source, 1 - core],
            dst_ref=whole_w.at[source, 1 - core],
            send_sem=ws_send.at[source],
            recv_sem=ws_recv.at[source],
            device_id={"dp": sibling},
            device_id_type=MESH,
        )

    to_slots(keys, 0, KV_COLS, send_block, tx[CH_K], rx[CH_K])
    to_slots(queries, 0, GROUP_COLS, send_block, tx[CH_Q], rx[CH_Q])
    pl.semaphore_wait(barrier, n_dp + n_f - 2)

    each(1, n_f, lambda i: w_copy(i).start())
    send_all(CH_K, tx[CH_K], rx[CH_K])
    send_all(CH_Q, tx[CH_Q], rx[CH_Q])
    for g in range(1, KV_HEADS):
        to_slots(queries, g * GROUP_COLS, GROUP_COLS, send_block, tx[CH_Q + g], rx[CH_Q + g])
        if g == 1:
            send_all(CH_Q + g, tx[CH_Q + g], rx[CH_Q + g])

    whole_w[f, 0] = weight[:half]
    whole_w[f, 1] = weight[half:]

    def transpose(c, _):
        at = pl.multiple_of(c * 256, 256)
        normed_t[pl.ds(at, 256), :] = normed[:, pl.ds(at, 256)].T
        return 0

    lax.fori_loop(0, width // 256, transpose, 0)

    docs_across = jnp.broadcast_to(doc_row[...], (TILE, rows))
    docs_down = docs_across.T
    for j in range(rows // TILE):
        same = docs_down == jnp.broadcast_to(doc_row[:, j * TILE : (j + 1) * TILE], (rows, TILE))
        i_at = lax.broadcasted_iota(jnp.int32, (rows, TILE), 0)
        j_at = lax.broadcasted_iota(jnp.int32, (rows, TILE), 1) + j * TILE
        bias[:, j * TILE : (j + 1) * TILE] = jnp.where(same & (j_at <= i_at), 0.0, MASKED)

    def add_values(i, first):
        at = f_peer(i)
        cols = normed[:, pl.ds(pl.multiple_of(at * shard, 128), shard)]
        term = jnp.dot(
            cols, whole_w[at].reshape(shard, KV_COLS), preferred_element_type=jnp.float32
        )
        values_f32[...] = term if first else values_f32[...] + term

    add_values(0, True)

    def forward(i):
        w_arrival(i).wait_recv()
        w_forward(i).start()

    each(1, n_f, forward)

    def later_values(i):
        w_forwarded(i).wait_recv()
        add_values(i, False)

    each(1, n_f, later_values)
    values[...] = values_f32[...].astype(jnp.bfloat16).reshape(values.shape)
    to_slots(values, 0, KV_COLS, send_block, tx[CH_V], rx[CH_V])
    send_all(CH_V, tx[CH_V], rx[CH_V])
    for g in range(2, KV_HEADS):
        send_all(CH_Q + g, tx[CH_Q + g], rx[CH_Q + g])

    recv_all(CH_K, tx[CH_K], rx[CH_K])
    from_slots(rx[CH_K], take_from, packed_k, 0, KV_COLS)

    scale = HEAD_DIM ** (-0.5)

    def attend(g):
        recv_all(CH_Q + g, tx[CH_Q + g], rx[CH_Q + g])
        from_slots(rx[CH_Q + g], take_from, packed_q, g * GROUP_COLS, GROUP_COLS)
        if g == 0:
            recv_all(CH_V, tx[CH_V], rx[CH_V])
            from_slots(rx[CH_V], take_from, packed_v, 0, KV_COLS)
        kv = slice(g * HEAD_DIM, (g + 1) * HEAD_DIM)
        for t in reversed(range(rows // TILE)):
            span = (t + 1) * TILE
            here = slice(t * TILE, span)
            heads = [
                slice(g * GROUP_COLS + x * HEAD_DIM, g * GROUP_COLS + (x + 1) * HEAD_DIM)
                for x in range(GROUP)
            ]
            q = jnp.concatenate([packed_q[here, h] for h in heads], axis=0)
            og = jnp.concatenate([out_grad[here, h] for h in heads], axis=0)
            k = packed_k[:span, kv]
            v = packed_v[:span, kv]
            s = lax.dot_general(q, k, NT, preferred_element_type=jnp.float32) * scale
            s = (s.reshape(GROUP, TILE, span) + bias[here, :span][None]).reshape(GROUP * TILE, span)
            peak = jnp.max(s, axis=-1, keepdims=True)
            e = jnp.exp(s - peak)
            p = e * (1.0 / jnp.sum(e, axis=-1, keepdims=True))
            ph = p.astype(jnp.bfloat16)
            pg = lax.dot_general(og, v, NT, preferred_element_type=jnp.float32)
            delta = jnp.sum(ph.astype(jnp.float32) * pg, axis=-1, keepdims=True)
            ds = (p * (pg - delta) * scale).astype(jnp.bfloat16)
            dq = jnp.dot(ds, k, preferred_element_type=jnp.float32).astype(jnp.bfloat16)
            for x, h in enumerate(heads):
                query_grad[here, h] = dq[x * TILE : (x + 1) * TILE]
            dk = lax.dot_general(ds, q, TN, preferred_element_type=jnp.float32)
            dv = lax.dot_general(ph, og, TN, preferred_element_type=jnp.float32)
            if span == rows:
                dk_acc[...] = dk
                dv_acc[...] = dv
            else:
                dk_acc[:span] += dk
                dv_acc[:span] += dv
        key_grad[:, kv] = dk_acc[...].astype(jnp.bfloat16)
        value_grad[:, :, kv] = dv_acc[...].astype(jnp.bfloat16).reshape(blocks, BLOCK_ROWS, HEAD_DIM)

    def return_values(h):
        to_slots(value_grad, h * HALF_COLS, HALF_COLS, take_block, gtx[h], grx[h])
        send_all(CH_G + h, gtx[h], grx[h])

    def pair_copy(h):
        return pltpu.make_async_remote_copy(
            src_ref=pair_tx.at[h],
            dst_ref=pair_rx.at[h],
            send_sem=p_send.at[h],
            recv_sem=p_recv.at[h],
            device_id={"dp": sibling},
            device_id_type=MESH,
        )

    def product(h, zz, which):
        at = pl.multiple_of((zz * 2 + which) * dest_rows, 128)
        return jnp.dot(
            normed_t[pl.ds(at, dest_rows), :], home[h], preferred_element_type=jnp.float32
        )

    def weight_terms(h):
        recv_all(CH_G + h, gtx[h], grx[h])
        for b in range(blocks):
            home[h, b * BLOCK_ROWS : (b + 1) * BLOCK_ROWS, :] = grx[h][send_to[0, b]]

        def other(zz):
            pair_tx[h, zz] = product(h, zz, 1 - core).astype(jnp.bfloat16)

        each(0, n_z, other)
        pair_copy(h).start()

    def f_copy(h, i):
        to = f_peer(i)
        return pltpu.make_async_remote_copy(
            src_ref=pair_sum.at[h, :, pl.ds(pl.multiple_of(to * piece, 16), piece)],
            dst_ref=f_rx.at[h, f],
            send_sem=f_send.at[h, to],
            recv_sem=f_recv.at[h, f],
            device_id={"fsdp": to},
            device_id_type=MESH,
        )

    def f_arrival(h, i):
        source = f_peer(i)
        return pltpu.make_async_remote_copy(
            src_ref=pair_sum.at[h, :, pl.ds(pl.multiple_of(source * piece, 16), piece)],
            dst_ref=f_rx.at[h, source],
            send_sem=f_send.at[h, source],
            recv_sem=f_recv.at[h, source],
            device_id={"fsdp": source},
            device_id_type=MESH,
        )

    def weight_pairs(h):
        pair_copy(h).wait_recv()

        def own(zz):
            total = product(h, zz, core) + pair_rx[h, zz].astype(jnp.float32)
            pair_sum[h, zz] = total.astype(jnp.bfloat16)

        each(0, n_z, own)
        each(1, n_f, lambda i: f_copy(h, i).start())

    def z_peer(i):
        return lax.rem(z + i, n_z)

    def z_copy(h, i):
        to = z_peer(i)
        return pltpu.make_async_remote_copy(
            src_ref=z_tx.at[h, to],
            dst_ref=z_rx.at[h, z],
            send_sem=z_send.at[h, to],
            recv_sem=z_recv.at[h, z],
            device_id={"dp": to * 2 + core},
            device_id_type=MESH,
        )

    def z_arrival(h, i):
        source = z_peer(i)
        return pltpu.make_async_remote_copy(
            src_ref=z_tx.at[h, source],
            dst_ref=z_rx.at[h, source],
            send_sem=z_send.at[h, source],
            recv_sem=z_recv.at[h, source],
            device_id={"dp": source * 2 + core},
            device_id_type=MESH,
        )

    def weight_squares(h):
        each(1, n_f, lambda i: f_arrival(h, i).wait_recv())
        mine = pl.multiple_of(f * piece, 16)

        def total(zz):
            acc = pair_sum[h, zz, pl.ds(mine, piece), :].astype(jnp.float32)
            for i in range(1, n_f):
                acc = acc + f_rx[h, f_peer(i), zz].astype(jnp.float32)
            z_tx[h, zz] = acc.astype(jnp.bfloat16)

        each(0, n_z, total)
        each(1, n_z, lambda i: z_copy(h, i).start())

    def weight_lines(h):
        each(1, n_z, lambda i: z_arrival(h, i).wait_recv())
        acc = z_tx[h, z].astype(jnp.float32)
        for i in range(1, n_z):
            acc = acc + z_rx[h, z_peer(i)].astype(jnp.float32)
        weight_grad[:, h * HALF_COLS : (h + 1) * HALF_COLS] = acc * grad_scale

    attend(0)
    attend(1)
    return_values(0)
    attend(2)
    weight_terms(0)
    attend(3)
    return_values(1)
    weight_pairs(0)

    def input_cols(at):
        w = whole_w[at].reshape(shard, KV_COLS)
        x = lax.dot_general(value_grad[...].reshape(rows, KV_COLS), w, NT, preferred_element_type=jnp.float32)
        input_grad[:, pl.ds(pl.multiple_of(at * shard, 128), shard)] = x.astype(jnp.bfloat16)

    weight_terms(1)
    each(0, n_f // 2, input_cols)
    weight_pairs(1)
    weight_squares(0)
    each(n_f // 2, n_f, input_cols)
    weight_squares(1)
    weight_lines(0)
    weight_lines(1)

    each(1, n_f, lambda i: w_copy(i).wait_send())
    each(1, n_f, lambda i: w_forward(i).wait_send())
    for channel in range(CH_G):
        each(1, n_dp, lambda i: exchange(channel, tx[channel], rx[channel], i).wait_send())
    for h in range(2):
        each(1, n_dp, lambda i: exchange(CH_G + h, gtx[h], grx[h], i).wait_send())
        pair_copy(h).wait_send()
        each(1, n_f, lambda i: f_copy(h, i).wait_send())
        each(1, n_z, lambda i: z_copy(h, i).wait_send())


def local(normed, queries, key_rows, out_grad, value_weight, doc_ids, send_to, take_from):
    n_dp = lax.axis_size("dp")
    n_f = lax.axis_size("fsdp")
    rows, width = normed.shape
    n_z = n_dp // 2
    shard = width // n_f
    dest_rows = width // n_dp
    piece = dest_rows // n_f
    half = jnp.bfloat16
    vmem = pl.BlockSpec(memory_space=pltpu.VMEM)
    smem = pl.BlockSpec(memory_space=pltpu.SMEM)
    dma = pltpu.SemaphoreType.DMA
    slots = [pltpu.VMEM((n_dp, BLOCK_ROWS, KV_COLS), half) for _ in range(CH_G)]
    half_slots = [pltpu.VMEM((n_dp, BLOCK_ROWS, HALF_COLS), half) for _ in range(2)]
    blocks = rows // BLOCK_ROWS
    lanes = jnp.arange(n_dp, dtype=jnp.int32)
    order = jnp.arange(blocks, dtype=jnp.int32)

    def inverse(table):
        return jnp.sum(
            jnp.where(table[:, :, None] == lanes, order[None, :, None], 0), axis=1, dtype=jnp.int32
        )

    return pl.pallas_call(
        functools.partial(kernel, n_dp, n_f, (rows * n_dp * n_f) ** (-0.5)),
        out_shape=(
            jax.ShapeDtypeStruct(queries.shape, half),
            jax.ShapeDtypeStruct(key_rows.shape, half),
            jax.ShapeDtypeStruct(normed.shape, half),
            jax.ShapeDtypeStruct((piece, KV_COLS), jnp.float32),
        ),
        in_specs=[vmem] * 6 + [smem] * 4,
        out_specs=(vmem,) * 4,
        scratch_shapes=[
            list(slots), list(slots), list(half_slots), list(half_slots),
            pltpu.VMEM((n_f, 2, shard // 2, KV_COLS), half),
            pltpu.VMEM((rows, KV_COLS), jnp.float32),
            pltpu.VMEM((rows // BLOCK_ROWS, BLOCK_ROWS, KV_COLS), half),
            pltpu.VMEM(queries.shape, half),
            pltpu.VMEM(key_rows.shape, half),
            pltpu.VMEM(key_rows.shape, half),
            pltpu.VMEM((width, rows), half),
            pltpu.VMEM((rows, rows), jnp.float32),
            pltpu.VMEM((rows, HEAD_DIM), jnp.float32),
            pltpu.VMEM((rows, HEAD_DIM), jnp.float32),
            pltpu.VMEM((rows // BLOCK_ROWS, BLOCK_ROWS, KV_COLS), half),
            pltpu.VMEM((2, rows, HALF_COLS), half),
            pltpu.VMEM((2, n_z, dest_rows, HALF_COLS), half),
            pltpu.VMEM((2, n_z, dest_rows, HALF_COLS), half),
            pltpu.VMEM((2, n_z, dest_rows, HALF_COLS), half),
            pltpu.VMEM((2, n_f, n_z, piece, HALF_COLS), half),
            pltpu.VMEM((2, n_z, piece, HALF_COLS), half),
            pltpu.VMEM((2, n_z, piece, HALF_COLS), half),
            dma((CH_G + 2, n_dp)), dma((CH_G + 2, n_dp)),
            dma((n_f,)), dma((n_f,)), dma((n_f,)), dma((n_f,)),
            dma((2,)), dma((2,)), dma((2, n_f)), dma((2, n_f)), dma((2, n_z)), dma((2, n_z)),
        ],
        compiler_params=pltpu.CompilerParams(
            collective_id=0, has_side_effects=True, vmem_limit_bytes=56 * 1024 * 1024
        ),
        cost_estimate=pl.CostEstimate(
            flops=10_000_000_000, bytes_accessed=16_000_000, transcendentals=2_400_000
        ),
        name="packed_backward",
    )(
        normed,
        queries.reshape(blocks, BLOCK_ROWS, queries.shape[1]),
        key_rows.reshape(blocks, BLOCK_ROWS, key_rows.shape[1]),
        out_grad, value_weight, doc_ids, send_to, take_from,
        inverse(send_to), inverse(take_from),
    )


def solution(mesh):
    rows = P(("dp", "fsdp"), None)
    return jax.shard_map(
        local,
        mesh=mesh,
        in_specs=(rows, rows, rows, rows, P("fsdp", None), rows, rows, rows),
        out_specs=(rows, rows, rows, rows),
        check_vma=False,
    )
```

```python
import functools

import jax
import jax.numpy as jnp
from jax import lax
from jax.experimental import pallas as pl
from jax.experimental.pallas import tpu as pltpu
from jax.sharding import PartitionSpec as P

HEADS = 16
KV_HEADS = 4
HEAD_DIM = 128
GROUP = HEADS // KV_HEADS
GROUP_COLS = GROUP * HEAD_DIM
KV_COLS = KV_HEADS * HEAD_DIM
BLOCK_ROWS = 48
TILE = 128
HALF_COLS = KV_COLS // 2
MASKED = -1e30
MESH = pl.DeviceIdType.MESH
CH_K, CH_V, CH_Q, CH_G = 0, 1, 2, 2 + KV_HEADS
NT = (((1,), (1,)), ((), ()))
TN = (((0,), (0,)), ((), ()))


def kernel(
    n_dp, n_f, grad_scale,
    normed, queries, keys, out_grad, weight, doc_row, send_to, take_from, send_block, take_block,
    query_grad, key_grad, input_grad, weight_grad,
    tx, rx, gtx, grx, whole_w, values_f32, values, packed_q, packed_k, packed_v,
    normed_t, bias, dk_acc, dv_acc, probs, value_grad, home, pair_tx, pair_rx, pair_sum,
    f_rx, z_tx, z_rx,
    a_send, a_recv, w_send, w_recv, ws_send, ws_recv, p_send, p_recv, f_send, f_recv,
    z_send, z_recv,
):
    rows, width = normed.shape
    blocks = rows // BLOCK_ROWS
    n_z = n_dp // 2
    shard = width // n_f
    half = shard // 2
    dest_rows = width // n_dp
    piece = dest_rows // n_f
    d = lax.axis_index("dp")
    f = lax.axis_index("fsdp")
    core = lax.rem(d, 2)
    z = lax.div(d, 2)
    sibling = d + 1 - 2 * core

    def dp_peer(i):
        return lax.rem(d + i, n_dp)

    def f_peer(i):
        return lax.rem(f + i, n_f)

    barrier = pltpu.get_barrier_semaphore()

    def greet_dp(i, _):
        pl.semaphore_signal(barrier, inc=1, device_id={"dp": dp_peer(i)}, device_id_type=MESH)
        return 0

    def greet_f(i, _):
        pl.semaphore_signal(barrier, inc=1, device_id={"fsdp": f_peer(i)}, device_id_type=MESH)
        return 0

    lax.fori_loop(1, n_dp, greet_dp, 0)
    lax.fori_loop(1, n_f, greet_f, 0)

    def to_slots(source, column, cols, table, out, own):
        def body(p, _):
            out[p] = source[table[0, p], :, column : column + cols]
            return 0

        lax.fori_loop(0, n_dp, body, 0)
        own[d] = out[d]

    def from_slots(landed, table, out, column, cols):
        for p in range(blocks):
            out[p * BLOCK_ROWS : (p + 1) * BLOCK_ROWS, column : column + cols] = landed[table[0, p]]

    def exchange(channel, out, landed, i):
        to = dp_peer(i)
        return pltpu.make_async_remote_copy(
            src_ref=out.at[to],
            dst_ref=landed.at[d],
            send_sem=a_send.at[channel, to],
            recv_sem=a_recv.at[channel, d],
            device_id={"dp": to},
            device_id_type=MESH,
        )

    def arrival(channel, out, landed, i):
        source = dp_peer(i)
        return pltpu.make_async_remote_copy(
            src_ref=out.at[source],
            dst_ref=landed.at[source],
            send_sem=a_send.at[channel, source],
            recv_sem=a_recv.at[channel, source],
            device_id={"dp": source},
            device_id_type=MESH,
        )

    def each(low, high, act):
        def body(i, _):
            act(i)
            return 0

        lax.fori_loop(low, high, body, 0)

    def send_all(channel, out, landed):
        each(1, n_dp, lambda i: exchange(channel, out, landed, i).start())

    def recv_all(channel, out, landed):
        each(1, n_dp, lambda i: arrival(channel, out, landed, i).wait_recv())

    def w_copy(i):
        to = f_peer(i)
        return pltpu.make_async_remote_copy(
            src_ref=weight.at[pl.ds(pl.multiple_of(core * half, 16), half)],
            dst_ref=whole_w.at[f, core],
            send_sem=w_send.at[to],
            recv_sem=w_recv.at[f],
            device_id={"fsdp": to},
            device_id_type=MESH,
        )

    def w_arrival(i):
        source = f_peer(i)
        return pltpu.make_async_remote_copy(
            src_ref=weight.at[pl.ds(pl.multiple_of(core * half, 16), half)],
            dst_ref=whole_w.at[source, core],
            send_sem=w_send.at[source],
            recv_sem=w_recv.at[source],
            device_id={"fsdp": source},
            device_id_type=MESH,
        )

    def w_forward(i):
        source = f_peer(i)
        return pltpu.make_async_remote_copy(
            src_ref=whole_w.at[source, core],
            dst_ref=whole_w.at[source, core],
            send_sem=ws_send.at[source],
            recv_sem=ws_recv.at[source],
            device_id={"dp": sibling},
            device_id_type=MESH,
        )

    def w_forwarded(i):
        source = f_peer(i)
        return pltpu.make_async_remote_copy(
            src_ref=whole_w.at[source, 1 - core],
            dst_ref=whole_w.at[source, 1 - core],
            send_sem=ws_send.at[source],
            recv_sem=ws_recv.at[source],
            device_id={"dp": sibling},
            device_id_type=MESH,
        )

    to_slots(keys, 0, KV_COLS, send_block, tx[CH_K], rx[CH_K])
    to_slots(queries, 0, GROUP_COLS, send_block, tx[CH_Q], rx[CH_Q])
    pl.semaphore_wait(barrier, n_dp + n_f - 2)

    each(1, n_f, lambda i: w_copy(i).start())
    send_all(CH_K, tx[CH_K], rx[CH_K])
    send_all(CH_Q, tx[CH_Q], rx[CH_Q])
    for g in range(1, KV_HEADS):
        to_slots(queries, g * GROUP_COLS, GROUP_COLS, send_block, tx[CH_Q + g], rx[CH_Q + g])
        send_all(CH_Q + g, tx[CH_Q + g], rx[CH_Q + g])

    whole_w[f, 0] = weight[:half]
    whole_w[f, 1] = weight[half:]

    def transpose(c, _):
        at = pl.multiple_of(c * 256, 256)
        normed_t[pl.ds(at, 256), :] = normed[:, pl.ds(at, 256)].T
        return 0

    lax.fori_loop(0, width // 256, transpose, 0)

    docs_across = jnp.broadcast_to(doc_row[...], (TILE, rows))
    docs_down = docs_across.T
    for j in range(rows // TILE):
        same = docs_down == jnp.broadcast_to(doc_row[:, j * TILE : (j + 1) * TILE], (rows, TILE))
        i_at = lax.broadcasted_iota(jnp.int32, (rows, TILE), 0)
        j_at = lax.broadcasted_iota(jnp.int32, (rows, TILE), 1) + j * TILE
        bias[:, j * TILE : (j + 1) * TILE] = jnp.where(same & (j_at <= i_at), 0.0, MASKED)

    def add_values(i, first):
        at = f_peer(i)
        cols = normed[:, pl.ds(pl.multiple_of(at * shard, 128), shard)]
        term = jnp.dot(
            cols, whole_w[at].reshape(shard, KV_COLS), preferred_element_type=jnp.float32
        )
        values_f32[...] = term if first else values_f32[...] + term

    def forward(i):
        w_arrival(i).wait_recv()
        w_forward(i).start()

    def later_values(i):
        w_forwarded(i).wait_recv()
        add_values(i, False)

    def make_values():
        add_values(0, True)
        each(1, n_f, later_values)
        values[...] = values_f32[...].astype(jnp.bfloat16).reshape(values.shape)
        to_slots(values, 0, KV_COLS, send_block, tx[CH_V], rx[CH_V])
        send_all(CH_V, tx[CH_V], rx[CH_V])

    scale = HEAD_DIM ** (-0.5)

    tiles = rows // TILE

    def head_cols(g):
        return [
            slice(g * GROUP_COLS + x * HEAD_DIM, g * GROUP_COLS + (x + 1) * HEAD_DIM)
            for x in range(GROUP)
        ]

    def stacked(ref, here, g):
        return jnp.concatenate([ref[here, h] for h in head_cols(g)], axis=0)

    def find_probs(g):
        recv_all(CH_Q + g, tx[CH_Q + g], rx[CH_Q + g])
        from_slots(rx[CH_Q + g], take_from, packed_q, g * GROUP_COLS, GROUP_COLS)
        kv = slice(g * HEAD_DIM, (g + 1) * HEAD_DIM)
        for t in reversed(range(tiles)):
            span = (t + 1) * TILE
            here = slice(t * TILE, span)
            q = stacked(packed_q, here, g)
            s = lax.dot_general(q, packed_k[:span, kv], NT, preferred_element_type=jnp.float32)
            s = (s * scale).reshape(GROUP, TILE, span) + bias[here, :span][None]
            s = s.reshape(GROUP * TILE, span)
            e = jnp.exp(s - jnp.max(s, axis=-1, keepdims=True))
            p = e * (1.0 / jnp.sum(e, axis=-1, keepdims=True))
            probs[g, t, :, :span] = p
            og = stacked(out_grad, here, g)
            dv = lax.dot_general(p.astype(jnp.bfloat16), og, TN, preferred_element_type=jnp.float32)
            if span == rows:
                dv_acc[...] = dv
            else:
                dv_acc[:span] += dv
        vg = dv_acc[...].astype(jnp.bfloat16)
        value_grad[:, :, kv] = vg.reshape(blocks, BLOCK_ROWS, HEAD_DIM)

    def find_grads(g):
        kv = slice(g * HEAD_DIM, (g + 1) * HEAD_DIM)
        for t in reversed(range(tiles)):
            span = (t + 1) * TILE
            here = slice(t * TILE, span)
            q = stacked(packed_q, here, g)
            og = stacked(out_grad, here, g)
            k = packed_k[:span, kv]
            v = packed_v[:span, kv]
            p = probs[g, t, :, :span]
            ph = p.astype(jnp.bfloat16)
            pg = lax.dot_general(og, v, NT, preferred_element_type=jnp.float32)
            delta = jnp.sum(ph.astype(jnp.float32) * pg, axis=-1, keepdims=True)
            ds = (p * (pg - delta) * scale).astype(jnp.bfloat16)
            dq = jnp.dot(ds, k, preferred_element_type=jnp.float32).astype(jnp.bfloat16)
            for x, h in enumerate(head_cols(g)):
                query_grad[here, h] = dq[x * TILE : (x + 1) * TILE]
            dk = lax.dot_general(ds, q, TN, preferred_element_type=jnp.float32)
            if span == rows:
                dk_acc[...] = dk
            else:
                dk_acc[:span] += dk
        key_grad[:, kv] = dk_acc[...].astype(jnp.bfloat16)

    def return_values(h):
        to_slots(value_grad, h * HALF_COLS, HALF_COLS, take_block, gtx[h], grx[h])
        send_all(CH_G + h, gtx[h], grx[h])

    def pair_copy(h):
        return pltpu.make_async_remote_copy(
            src_ref=pair_tx.at[h],
            dst_ref=pair_rx.at[h],
            send_sem=p_send.at[h],
            recv_sem=p_recv.at[h],
            device_id={"dp": sibling},
            device_id_type=MESH,
        )

    def product(h, zz, which):
        at = pl.multiple_of((zz * 2 + which) * dest_rows, 128)
        return jnp.dot(
            normed_t[pl.ds(at, dest_rows), :], home[h], preferred_element_type=jnp.float32
        )

    def weight_terms(h):
        recv_all(CH_G + h, gtx[h], grx[h])
        for b in range(blocks):
            home[h, b * BLOCK_ROWS : (b + 1) * BLOCK_ROWS, :] = grx[h][send_to[0, b]]

        def other(zz):
            pair_tx[h, zz] = product(h, zz, 1 - core).astype(jnp.bfloat16)

        each(0, n_z, other)
        pair_copy(h).start()

    def f_copy(h, i):
        to = f_peer(i)
        return pltpu.make_async_remote_copy(
            src_ref=pair_sum.at[h, :, pl.ds(pl.multiple_of(to * piece, 16), piece)],
            dst_ref=f_rx.at[h, f],
            send_sem=f_send.at[h, to],
            recv_sem=f_recv.at[h, f],
            device_id={"fsdp": to},
            device_id_type=MESH,
        )

    def f_arrival(h, i):
        source = f_peer(i)
        return pltpu.make_async_remote_copy(
            src_ref=pair_sum.at[h, :, pl.ds(pl.multiple_of(source * piece, 16), piece)],
            dst_ref=f_rx.at[h, source],
            send_sem=f_send.at[h, source],
            recv_sem=f_recv.at[h, source],
            device_id={"fsdp": source},
            device_id_type=MESH,
        )

    def weight_pairs(h):
        pair_copy(h).wait_recv()

        def own(zz):
            total = product(h, zz, core) + pair_rx[h, zz].astype(jnp.float32)
            pair_sum[h, zz] = total.astype(jnp.bfloat16)

        each(0, n_z, own)
        each(1, n_f, lambda i: f_copy(h, i).start())

    def z_peer(i):
        return lax.rem(z + i, n_z)

    def z_copy(h, i):
        to = z_peer(i)
        return pltpu.make_async_remote_copy(
            src_ref=z_tx.at[h, to],
            dst_ref=z_rx.at[h, z],
            send_sem=z_send.at[h, to],
            recv_sem=z_recv.at[h, z],
            device_id={"dp": to * 2 + core},
            device_id_type=MESH,
        )

    def z_arrival(h, i):
        source = z_peer(i)
        return pltpu.make_async_remote_copy(
            src_ref=z_tx.at[h, source],
            dst_ref=z_rx.at[h, source],
            send_sem=z_send.at[h, source],
            recv_sem=z_recv.at[h, source],
            device_id={"dp": source * 2 + core},
            device_id_type=MESH,
        )

    def weight_squares(h):
        each(1, n_f, lambda i: f_arrival(h, i).wait_recv())
        mine = pl.multiple_of(f * piece, 16)

        def total(zz):
            acc = pair_sum[h, zz, pl.ds(mine, piece), :].astype(jnp.float32)
            for i in range(1, n_f):
                acc = acc + f_rx[h, f_peer(i), zz].astype(jnp.float32)
            z_tx[h, zz] = acc.astype(jnp.bfloat16)

        each(0, n_z, total)
        each(1, n_z, lambda i: z_copy(h, i).start())

    def weight_lines(h):
        each(1, n_z, lambda i: z_arrival(h, i).wait_recv())
        acc = z_tx[h, z].astype(jnp.float32)
        for i in range(1, n_z):
            acc = acc + z_rx[h, z_peer(i)].astype(jnp.float32)
        weight_grad[:, h * HALF_COLS : (h + 1) * HALF_COLS] = acc * grad_scale

    def input_cols(at):
        w = whole_w[at].reshape(shard, KV_COLS)
        vg = value_grad[...].reshape(rows, KV_COLS)
        x = lax.dot_general(vg, w, NT, preferred_element_type=jnp.float32)
        input_grad[:, pl.ds(pl.multiple_of(at * shard, 128), shard)] = x.astype(jnp.bfloat16)

    recv_all(CH_K, tx[CH_K], rx[CH_K])
    from_slots(rx[CH_K], take_from, packed_k, 0, KV_COLS)
    find_probs(0)
    find_probs(1)
    return_values(0)
    each(1, n_f, forward)
    find_probs(2)
    make_values()
    weight_terms(0)
    find_probs(3)
    return_values(1)
    weight_pairs(0)
    each(0, n_f, input_cols)
    weight_terms(1)
    recv_all(CH_V, tx[CH_V], rx[CH_V])
    from_slots(rx[CH_V], take_from, packed_v, 0, KV_COLS)
    weight_pairs(1)
    weight_squares(0)
    find_grads(0)
    find_grads(1)
    find_grads(2)
    weight_squares(1)
    find_grads(3)
    weight_lines(0)
    weight_lines(1)

    each(1, n_f, lambda i: w_copy(i).wait_send())
    each(1, n_f, lambda i: w_forward(i).wait_send())
    for channel in range(CH_G):
        each(1, n_dp, lambda i: exchange(channel, tx[channel], rx[channel], i).wait_send())
    for h in range(2):
        each(1, n_dp, lambda i: exchange(CH_G + h, gtx[h], grx[h], i).wait_send())
        pair_copy(h).wait_send()
        each(1, n_f, lambda i: f_copy(h, i).wait_send())
        each(1, n_z, lambda i: z_copy(h, i).wait_send())


def local(normed, queries, key_rows, out_grad, value_weight, doc_ids, send_to, take_from):
    n_dp = lax.axis_size("dp")
    n_f = lax.axis_size("fsdp")
    rows, width = normed.shape
    n_z = n_dp // 2
    shard = width // n_f
    dest_rows = width // n_dp
    piece = dest_rows // n_f
    half = jnp.bfloat16
    vmem = pl.BlockSpec(memory_space=pltpu.VMEM)
    smem = pl.BlockSpec(memory_space=pltpu.SMEM)
    dma = pltpu.SemaphoreType.DMA
    slots = [pltpu.VMEM((n_dp, BLOCK_ROWS, KV_COLS), half) for _ in range(CH_G)]
    half_slots = [pltpu.VMEM((n_dp, BLOCK_ROWS, HALF_COLS), half) for _ in range(2)]
    blocks = rows // BLOCK_ROWS
    lanes = jnp.arange(n_dp, dtype=jnp.int32)
    order = jnp.arange(blocks, dtype=jnp.int32)

    def inverse(table):
        return jnp.sum(
            jnp.where(table[:, :, None] == lanes, order[None, :, None], 0), axis=1, dtype=jnp.int32
        )

    return pl.pallas_call(
        functools.partial(kernel, n_dp, n_f, (rows * n_dp * n_f) ** (-0.5)),
        out_shape=(
            jax.ShapeDtypeStruct(queries.shape, half),
            jax.ShapeDtypeStruct(key_rows.shape, half),
            jax.ShapeDtypeStruct(normed.shape, half),
            jax.ShapeDtypeStruct((piece, KV_COLS), jnp.float32),
        ),
        in_specs=[vmem] * 6 + [smem] * 4,
        out_specs=(vmem,) * 4,
        scratch_shapes=[
            list(slots), list(slots), list(half_slots), list(half_slots),
            pltpu.VMEM((n_f, 2, shard // 2, KV_COLS), half),
            pltpu.VMEM((rows, KV_COLS), jnp.float32),
            pltpu.VMEM((rows // BLOCK_ROWS, BLOCK_ROWS, KV_COLS), half),
            pltpu.VMEM(queries.shape, half),
            pltpu.VMEM(key_rows.shape, half),
            pltpu.VMEM(key_rows.shape, half),
            pltpu.VMEM((width, rows), half),
            pltpu.VMEM((rows, rows), jnp.float32),
            pltpu.VMEM((rows, HEAD_DIM), jnp.float32),
            pltpu.VMEM((rows, HEAD_DIM), jnp.float32),
            pltpu.VMEM((KV_HEADS, rows // TILE, GROUP * TILE, rows), jnp.float32),
            pltpu.VMEM((rows // BLOCK_ROWS, BLOCK_ROWS, KV_COLS), half),
            pltpu.VMEM((2, rows, HALF_COLS), half),
            pltpu.VMEM((2, n_z, dest_rows, HALF_COLS), half),
            pltpu.VMEM((2, n_z, dest_rows, HALF_COLS), half),
            pltpu.VMEM((2, n_z, dest_rows, HALF_COLS), half),
            pltpu.VMEM((2, n_f, n_z, piece, HALF_COLS), half),
            pltpu.VMEM((2, n_z, piece, HALF_COLS), half),
            pltpu.VMEM((2, n_z, piece, HALF_COLS), half),
            dma((CH_G + 2, n_dp)), dma((CH_G + 2, n_dp)),
            dma((n_f,)), dma((n_f,)), dma((n_f,)), dma((n_f,)),
            dma((2,)), dma((2,)), dma((2, n_f)), dma((2, n_f)), dma((2, n_z)), dma((2, n_z)),
        ],
        compiler_params=pltpu.CompilerParams(
            collective_id=0, has_side_effects=True, vmem_limit_bytes=42 * 1024 * 1024
        ),
        cost_estimate=pl.CostEstimate(
            flops=10_000_000_000, bytes_accessed=16_000_000, transcendentals=2_400_000
        ),
        name="packed_backward",
    )(
        normed,
        queries.reshape(blocks, BLOCK_ROWS, queries.shape[1]),
        key_rows.reshape(blocks, BLOCK_ROWS, key_rows.shape[1]),
        out_grad, value_weight, doc_ids, send_to, take_from,
        inverse(send_to), inverse(take_from),
    )


def solution(mesh):
    rows = P(("dp", "fsdp"), None)
    return jax.shard_map(
        local,
        mesh=mesh,
        in_specs=(rows, rows, rows, rows, P("fsdp", None), rows, rows, rows),
        out_specs=(rows, rows, rows, rows),
        check_vma=False,
    )
```

```python
import functools

import jax
import jax.numpy as jnp
from jax import lax
from jax.experimental import pallas as pl
from jax.experimental.pallas import tpu as pltpu
from jax.sharding import PartitionSpec as P

HEADS = 16
KV_HEADS = 4
HEAD_DIM = 128
GROUP = HEADS // KV_HEADS
GROUP_COLS = GROUP * HEAD_DIM
KV_COLS = KV_HEADS * HEAD_DIM
BLOCK_ROWS = 48
TILE = 128
HALF_COLS = KV_COLS // 2
MASKED = -1e30
MESH = pl.DeviceIdType.MESH
CH_K, CH_V, CH_Q, CH_G = 0, 1, 2, 2 + KV_HEADS
NT = (((1,), (1,)), ((), ()))
TN = (((0,), (0,)), ((), ()))


def kernel(
    n_dp, n_f, grad_scale,
    normed_in, queries_in, keys_in, out_grad_in, weight_in, doc_row, send_to, take_from, send_block, take_block,
    query_grad, key_grad, input_grad, weight_grad,
    normed, queries, keys, out_grad, weight, in_sem,
    tx, rx, gtx, grx, whole_w, values_f32, values, packed_q, packed_k, packed_v,
    normed_t, bias, dk_acc, dv_acc, probs, value_grad, home, pair_tx, pair_rx, pair_sum,
    f_rx, z_tx, z_rx,
    a_send, a_recv, w_send, w_recv, ws_send, ws_recv, p_send, p_recv, f_send, f_recv,
    z_send, z_recv,
):
    rows, width = normed.shape
    blocks = rows // BLOCK_ROWS
    n_z = n_dp // 2
    shard = width // n_f
    half = shard // 2
    dest_rows = width // n_dp
    piece = dest_rows // n_f
    d = lax.axis_index("dp")
    f = lax.axis_index("fsdp")
    core = lax.rem(d, 2)
    z = lax.div(d, 2)
    sibling = d + 1 - 2 * core

    def dp_peer(i):
        return lax.rem(d + i, n_dp)

    def f_peer(i):
        return lax.rem(f + i, n_f)

    def load(at, source, out):
        copy = pltpu.make_async_copy(source, out, in_sem.at[at])
        copy.start()
        return copy

    keys_load = load(0, keys_in, keys)
    queries_load = load(1, queries_in, queries)
    weight_load = load(2, weight_in, weight)
    normed_load = load(3, normed_in, normed)
    out_grad_load = load(4, out_grad_in, out_grad)

    barrier = pltpu.get_barrier_semaphore()

    def greet_dp(i, _):
        pl.semaphore_signal(barrier, inc=1, device_id={"dp": dp_peer(i)}, device_id_type=MESH)
        return 0

    def greet_f(i, _):
        pl.semaphore_signal(barrier, inc=1, device_id={"fsdp": f_peer(i)}, device_id_type=MESH)
        return 0

    lax.fori_loop(1, n_dp, greet_dp, 0)
    lax.fori_loop(1, n_f, greet_f, 0)

    def to_slots(source, column, cols, table, out, own):
        def body(p, _):
            out[p] = source[table[0, p], :, column : column + cols]
            return 0

        lax.fori_loop(0, n_dp, body, 0)
        own[d] = out[d]

    def from_slots(landed, table, out, column, cols):
        for p in range(blocks):
            out[p * BLOCK_ROWS : (p + 1) * BLOCK_ROWS, column : column + cols] = landed[table[0, p]]

    def exchange(channel, out, landed, i):
        to = dp_peer(i)
        return pltpu.make_async_remote_copy(
            src_ref=out.at[to],
            dst_ref=landed.at[d],
            send_sem=a_send.at[channel, to],
            recv_sem=a_recv.at[channel, d],
            device_id={"dp": to},
            device_id_type=MESH,
        )

    def arrival(channel, out, landed, i):
        source = dp_peer(i)
        return pltpu.make_async_remote_copy(
            src_ref=out.at[source],
            dst_ref=landed.at[source],
            send_sem=a_send.at[channel, source],
            recv_sem=a_recv.at[channel, source],
            device_id={"dp": source},
            device_id_type=MESH,
        )

    def each(low, high, act):
        def body(i, _):
            act(i)
            return 0

        lax.fori_loop(low, high, body, 0)

    def send_all(channel, out, landed):
        each(1, n_dp, lambda i: exchange(channel, out, landed, i).start())

    def recv_all(channel, out, landed):
        each(1, n_dp, lambda i: arrival(channel, out, landed, i).wait_recv())

    def w_copy(i):
        to = f_peer(i)
        return pltpu.make_async_remote_copy(
            src_ref=weight.at[pl.ds(pl.multiple_of(core * half, 16), half)],
            dst_ref=whole_w.at[f, core],
            send_sem=w_send.at[to],
            recv_sem=w_recv.at[f],
            device_id={"fsdp": to},
            device_id_type=MESH,
        )

    def w_arrival(i):
        source = f_peer(i)
        return pltpu.make_async_remote_copy(
            src_ref=weight.at[pl.ds(pl.multiple_of(core * half, 16), half)],
            dst_ref=whole_w.at[source, core],
            send_sem=w_send.at[source],
            recv_sem=w_recv.at[source],
            device_id={"fsdp": source},
            device_id_type=MESH,
        )

    def w_forward(i):
        source = f_peer(i)
        return pltpu.make_async_remote_copy(
            src_ref=whole_w.at[source, core],
            dst_ref=whole_w.at[source, core],
            send_sem=ws_send.at[source],
            recv_sem=ws_recv.at[source],
            device_id={"dp": sibling},
            device_id_type=MESH,
        )

    def w_forwarded(i):
        source = f_peer(i)
        return pltpu.make_async_remote_copy(
            src_ref=whole_w.at[source, 1 - core],
            dst_ref=whole_w.at[source, 1 - core],
            send_sem=ws_send.at[source],
            recv_sem=ws_recv.at[source],
            device_id={"dp": sibling},
            device_id_type=MESH,
        )

    keys_load.wait()
    to_slots(keys, 0, KV_COLS, send_block, tx[CH_K], rx[CH_K])
    queries_load.wait()
    to_slots(queries, 0, GROUP_COLS, send_block, tx[CH_Q], rx[CH_Q])
    weight_load.wait()
    pl.semaphore_wait(barrier, n_dp + n_f - 2)

    each(1, n_f, lambda i: w_copy(i).start())
    send_all(CH_K, tx[CH_K], rx[CH_K])
    send_all(CH_Q, tx[CH_Q], rx[CH_Q])
    for g in range(1, KV_HEADS):
        to_slots(queries, g * GROUP_COLS, GROUP_COLS, send_block, tx[CH_Q + g], rx[CH_Q + g])
        send_all(CH_Q + g, tx[CH_Q + g], rx[CH_Q + g])

    normed_load.wait()
    out_grad_load.wait()
    whole_w[f, 0] = weight[:half]
    whole_w[f, 1] = weight[half:]

    def transpose(c, _):
        at = pl.multiple_of(c * 256, 256)
        normed_t[pl.ds(at, 256), :] = normed[:, pl.ds(at, 256)].T
        return 0

    lax.fori_loop(0, width // 256, transpose, 0)

    docs_across = jnp.broadcast_to(doc_row[...], (TILE, rows))
    docs_down = docs_across.T
    for j in range(rows // TILE):
        same = docs_down == jnp.broadcast_to(doc_row[:, j * TILE : (j + 1) * TILE], (rows, TILE))
        i_at = lax.broadcasted_iota(jnp.int32, (rows, TILE), 0)
        j_at = lax.broadcasted_iota(jnp.int32, (rows, TILE), 1) + j * TILE
        bias[:, j * TILE : (j + 1) * TILE] = jnp.where(same & (j_at <= i_at), 0.0, MASKED)

    def add_values(i, first):
        at = f_peer(i)
        cols = normed[:, pl.ds(pl.multiple_of(at * shard, 128), shard)]
        term = jnp.dot(
            cols, whole_w[at].reshape(shard, KV_COLS), preferred_element_type=jnp.float32
        )
        values_f32[...] = term if first else values_f32[...] + term

    def forward(i):
        w_arrival(i).wait_recv()
        w_forward(i).start()

    def later_values(i):
        w_forwarded(i).wait_recv()
        add_values(i, False)

    def make_values():
        add_values(0, True)
        each(1, n_f, later_values)
        values[...] = values_f32[...].astype(jnp.bfloat16).reshape(values.shape)

    def send_values():
        to_slots(values, 0, KV_COLS, send_block, tx[CH_V], rx[CH_V])
        send_all(CH_V, tx[CH_V], rx[CH_V])

    scale = HEAD_DIM ** (-0.5)

    tiles = rows // TILE

    def head_cols(g):
        return [
            slice(g * GROUP_COLS + x * HEAD_DIM, g * GROUP_COLS + (x + 1) * HEAD_DIM)
            for x in range(GROUP)
        ]

    def stacked(ref, here, g):
        return jnp.concatenate([ref[here, h] for h in head_cols(g)], axis=0)

    def find_probs(g):
        recv_all(CH_Q + g, tx[CH_Q + g], rx[CH_Q + g])
        from_slots(rx[CH_Q + g], take_from, packed_q, g * GROUP_COLS, GROUP_COLS)
        kv = slice(g * HEAD_DIM, (g + 1) * HEAD_DIM)
        for t in reversed(range(tiles)):
            span = (t + 1) * TILE
            here = slice(t * TILE, span)
            q = stacked(packed_q, here, g)
            s = lax.dot_general(q, packed_k[:span, kv], NT, preferred_element_type=jnp.float32)
            s = (s * scale).reshape(GROUP, TILE, span) + bias[here, :span][None]
            s = s.reshape(GROUP * TILE, span)
            e = jnp.exp(s - jnp.max(s, axis=-1, keepdims=True))
            p = e * (1.0 / jnp.sum(e, axis=-1, keepdims=True))
            probs[g, t, :, :span] = p
            og = stacked(out_grad, here, g)
            dv = lax.dot_general(p.astype(jnp.bfloat16), og, TN, preferred_element_type=jnp.float32)
            if span == rows:
                dv_acc[...] = dv
            else:
                dv_acc[:span] += dv
        vg = dv_acc[...].astype(jnp.bfloat16)
        value_grad[:, :, kv] = vg.reshape(blocks, BLOCK_ROWS, HEAD_DIM)

    def find_grads(g):
        kv = slice(g * HEAD_DIM, (g + 1) * HEAD_DIM)
        for t in reversed(range(tiles)):
            span = (t + 1) * TILE
            here = slice(t * TILE, span)
            q = stacked(packed_q, here, g)
            og = stacked(out_grad, here, g)
            k = packed_k[:span, kv]
            v = packed_v[:span, kv]
            p = probs[g, t, :, :span]
            ph = p.astype(jnp.bfloat16)
            pg = lax.dot_general(og, v, NT, preferred_element_type=jnp.float32)
            delta = jnp.sum(ph.astype(jnp.float32) * pg, axis=-1, keepdims=True)
            ds = (p * (pg - delta) * scale).astype(jnp.bfloat16)
            dq = jnp.dot(ds, k, preferred_element_type=jnp.float32).astype(jnp.bfloat16)
            for x, h in enumerate(head_cols(g)):
                query_grad[here, h] = dq[x * TILE : (x + 1) * TILE]
            dk = lax.dot_general(ds, q, TN, preferred_element_type=jnp.float32)
            if span == rows:
                dk_acc[...] = dk
            else:
                dk_acc[:span] += dk
        key_grad[:, kv] = dk_acc[...].astype(jnp.bfloat16)

    def return_values(h):
        to_slots(value_grad, h * HALF_COLS, HALF_COLS, take_block, gtx[h], grx[h])
        send_all(CH_G + h, gtx[h], grx[h])

    def pair_copy(h):
        return pltpu.make_async_remote_copy(
            src_ref=pair_tx.at[h],
            dst_ref=pair_rx.at[h],
            send_sem=p_send.at[h],
            recv_sem=p_recv.at[h],
            device_id={"dp": sibling},
            device_id_type=MESH,
        )

    def product(h, zz, which):
        at = pl.multiple_of((zz * 2 + which) * dest_rows, 128)
        return jnp.dot(
            normed_t[pl.ds(at, dest_rows), :], home[h], preferred_element_type=jnp.float32
        )

    def weight_terms(h):
        recv_all(CH_G + h, gtx[h], grx[h])
        for b in range(blocks):
            home[h, b * BLOCK_ROWS : (b + 1) * BLOCK_ROWS, :] = grx[h][send_to[0, b]]

        def other(zz):
            pair_tx[h, zz] = product(h, zz, 1 - core).astype(jnp.bfloat16)

        each(0, n_z, other)
        pair_copy(h).start()

    def f_copy(h, i):
        to = f_peer(i)
        return pltpu.make_async_remote_copy(
            src_ref=pair_sum.at[h, :, pl.ds(pl.multiple_of(to * piece, 16), piece)],
            dst_ref=f_rx.at[h, f],
            send_sem=f_send.at[h, to],
            recv_sem=f_recv.at[h, f],
            device_id={"fsdp": to},
            device_id_type=MESH,
        )

    def f_arrival(h, i):
        source = f_peer(i)
        return pltpu.make_async_remote_copy(
            src_ref=pair_sum.at[h, :, pl.ds(pl.multiple_of(source * piece, 16), piece)],
            dst_ref=f_rx.at[h, source],
            send_sem=f_send.at[h, source],
            recv_sem=f_recv.at[h, source],
            device_id={"fsdp": source},
            device_id_type=MESH,
        )

    def weight_pairs(h):
        pair_copy(h).wait_recv()

        def own(zz):
            total = product(h, zz, core) + pair_rx[h, zz].astype(jnp.float32)
            pair_sum[h, zz] = total.astype(jnp.bfloat16)

        each(0, n_z, own)
        each(1, n_f, lambda i: f_copy(h, i).start())

    def z_peer(i):
        return lax.rem(z + i, n_z)

    def z_copy(h, i):
        to = z_peer(i)
        return pltpu.make_async_remote_copy(
            src_ref=z_tx.at[h, to],
            dst_ref=z_rx.at[h, z],
            send_sem=z_send.at[h, to],
            recv_sem=z_recv.at[h, z],
            device_id={"dp": to * 2 + core},
            device_id_type=MESH,
        )

    def z_arrival(h, i):
        source = z_peer(i)
        return pltpu.make_async_remote_copy(
            src_ref=z_tx.at[h, source],
            dst_ref=z_rx.at[h, source],
            send_sem=z_send.at[h, source],
            recv_sem=z_recv.at[h, source],
            device_id={"dp": source * 2 + core},
            device_id_type=MESH,
        )

    def weight_squares(h):
        each(1, n_f, lambda i: f_arrival(h, i).wait_recv())
        mine = pl.multiple_of(f * piece, 16)

        def total(zz):
            acc = pair_sum[h, zz, pl.ds(mine, piece), :].astype(jnp.float32)
            for i in range(1, n_f):
                acc = acc + f_rx[h, f_peer(i), zz].astype(jnp.float32)
            z_tx[h, zz] = acc.astype(jnp.bfloat16)

        each(0, n_z, total)
        each(1, n_z, lambda i: z_copy(h, i).start())

    def weight_lines(h):
        each(1, n_z, lambda i: z_arrival(h, i).wait_recv())
        acc = z_tx[h, z].astype(jnp.float32)
        for i in range(1, n_z):
            acc = acc + z_rx[h, z_peer(i)].astype(jnp.float32)
        weight_grad[:, h * HALF_COLS : (h + 1) * HALF_COLS] = acc * grad_scale

    def input_cols(at):
        w = whole_w[at].reshape(shard, KV_COLS)
        vg = value_grad[...].reshape(rows, KV_COLS)
        x = lax.dot_general(vg, w, NT, preferred_element_type=jnp.float32)
        input_grad[:, pl.ds(pl.multiple_of(at * shard, 128), shard)] = x.astype(jnp.bfloat16)

    recv_all(CH_K, tx[CH_K], rx[CH_K])
    from_slots(rx[CH_K], take_from, packed_k, 0, KV_COLS)
    find_probs(0)
    find_probs(1)
    return_values(0)
    each(1, n_f, forward)
    find_probs(2)
    make_values()
    find_probs(3)
    return_values(1)
    send_values()
    weight_terms(0)
    each(0, n_f // 2, input_cols)
    weight_pairs(0)
    weight_terms(1)
    each(n_f // 2, n_f, input_cols)
    weight_pairs(1)
    weight_squares(0)
    recv_all(CH_V, tx[CH_V], rx[CH_V])
    from_slots(rx[CH_V], take_from, packed_v, 0, KV_COLS)
    find_grads(0)
    find_grads(1)
    weight_squares(1)
    find_grads(2)
    find_grads(3)
    weight_lines(0)
    weight_lines(1)

    each(1, n_f, lambda i: w_copy(i).wait_send())
    each(1, n_f, lambda i: w_forward(i).wait_send())
    for channel in range(CH_G):
        each(1, n_dp, lambda i: exchange(channel, tx[channel], rx[channel], i).wait_send())
    for h in range(2):
        each(1, n_dp, lambda i: exchange(CH_G + h, gtx[h], grx[h], i).wait_send())
        pair_copy(h).wait_send()
        each(1, n_f, lambda i: f_copy(h, i).wait_send())
        each(1, n_z, lambda i: z_copy(h, i).wait_send())


def local(normed, queries, key_rows, out_grad, value_weight, doc_ids, send_to, take_from):
    n_dp = lax.axis_size("dp")
    n_f = lax.axis_size("fsdp")
    rows, width = normed.shape
    n_z = n_dp // 2
    shard = width // n_f
    dest_rows = width // n_dp
    piece = dest_rows // n_f
    half = jnp.bfloat16
    vmem = pl.BlockSpec(memory_space=pltpu.VMEM)
    smem = pl.BlockSpec(memory_space=pltpu.SMEM)
    hbm = pl.BlockSpec(memory_space=pltpu.HBM)
    dma = pltpu.SemaphoreType.DMA
    slots = [pltpu.VMEM((n_dp, BLOCK_ROWS, KV_COLS), half) for _ in range(CH_G)]
    half_slots = [pltpu.VMEM((n_dp, BLOCK_ROWS, HALF_COLS), half) for _ in range(2)]
    blocks = rows // BLOCK_ROWS
    lanes = jnp.arange(n_dp, dtype=jnp.int32)
    order = jnp.arange(blocks, dtype=jnp.int32)

    def inverse(table):
        return jnp.sum(
            jnp.where(table[:, :, None] == lanes, order[None, :, None], 0), axis=1, dtype=jnp.int32
        )

    return pl.pallas_call(
        functools.partial(kernel, n_dp, n_f, (rows * n_dp * n_f) ** (-0.5)),
        out_shape=(
            jax.ShapeDtypeStruct(queries.shape, half),
            jax.ShapeDtypeStruct(key_rows.shape, half),
            jax.ShapeDtypeStruct(normed.shape, half),
            jax.ShapeDtypeStruct((piece, KV_COLS), jnp.float32),
        ),
        in_specs=[hbm] * 5 + [vmem] + [smem] * 4,
        out_specs=(vmem,) * 4,
        scratch_shapes=[
            pltpu.VMEM(normed.shape, half),
            pltpu.VMEM((blocks, BLOCK_ROWS, queries.shape[1]), half),
            pltpu.VMEM((blocks, BLOCK_ROWS, key_rows.shape[1]), half),
            pltpu.VMEM(out_grad.shape, half),
            pltpu.VMEM(value_weight.shape, half),
            dma((5,)),
            list(slots), list(slots), list(half_slots), list(half_slots),
            pltpu.VMEM((n_f, 2, shard // 2, KV_COLS), half),
            pltpu.VMEM((rows, KV_COLS), jnp.float32),
            pltpu.VMEM((rows // BLOCK_ROWS, BLOCK_ROWS, KV_COLS), half),
            pltpu.VMEM(queries.shape, half),
            pltpu.VMEM(key_rows.shape, half),
            pltpu.VMEM(key_rows.shape, half),
            pltpu.VMEM((width, rows), half),
            pltpu.VMEM((rows, rows), jnp.float32),
            pltpu.VMEM((rows, HEAD_DIM), jnp.float32),
            pltpu.VMEM((rows, HEAD_DIM), jnp.float32),
            pltpu.VMEM((KV_HEADS, rows // TILE, GROUP * TILE, rows), jnp.float32),
            pltpu.VMEM((rows // BLOCK_ROWS, BLOCK_ROWS, KV_COLS), half),
            pltpu.VMEM((2, rows, HALF_COLS), half),
            pltpu.VMEM((2, n_z, dest_rows, HALF_COLS), half),
            pltpu.VMEM((2, n_z, dest_rows, HALF_COLS), half),
            pltpu.VMEM((2, n_z, dest_rows, HALF_COLS), half),
            pltpu.VMEM((2, n_f, n_z, piece, HALF_COLS), half),
            pltpu.VMEM((2, n_z, piece, HALF_COLS), half),
            pltpu.VMEM((2, n_z, piece, HALF_COLS), half),
            dma((CH_G + 2, n_dp)), dma((CH_G + 2, n_dp)),
            dma((n_f,)), dma((n_f,)), dma((n_f,)), dma((n_f,)),
            dma((2,)), dma((2,)), dma((2, n_f)), dma((2, n_f)), dma((2, n_z)), dma((2, n_z)),
        ],
        compiler_params=pltpu.CompilerParams(
            collective_id=0, has_side_effects=True, vmem_limit_bytes=53 * 1024 * 1024
        ),
        cost_estimate=pl.CostEstimate(
            flops=10_000_000_000, bytes_accessed=16_000_000, transcendentals=2_400_000
        ),
        name="packed_backward",
    )(
        normed,
        queries.reshape(blocks, BLOCK_ROWS, queries.shape[1]),
        key_rows.reshape(blocks, BLOCK_ROWS, key_rows.shape[1]),
        out_grad, value_weight, doc_ids, send_to, take_from,
        inverse(send_to), inverse(take_from),
    )


def solution(mesh):
    rows = P(("dp", "fsdp"), None)
    return jax.shard_map(
        local,
        mesh=mesh,
        in_specs=(rows, rows, rows, rows, P("fsdp", None), rows, rows, rows),
        out_specs=(rows, rows, rows, rows),
        check_vma=False,
    )
```
